32 devices in a mesh: quad: 16 (over z, x, core), rows: 2 (over y).
Axes of the slice: x: 2, y: 2, z: 4, core: 2. Of those that a mesh axis runs over, the one named last changes fastest.
Arguments:
- solutions: bfloat16 [32, 2, 64, 16, 1280], P('quad', None, None, None, 'rows'), may hold values from -64 to 64
- angles: float32 [32], replicated, may hold values from -3.140625 to 3.140625
- qweights: float32 [2, 32], replicated, may hold values from -1 to 1
- neighbours: int32 [320, 8], P(('quad', 'rows')), may hold values from 0 to 319, as said below
- hblocks: bfloat16 [320, 64, 512], P(('quad', 'rows')), may hold values from -0.25 to 0.25
Outputs:
- h_moments: bfloat16 [1024, 20480], P(None, ('quad', 'rows'))
- ritz_matrices: float32 [512, 2, 2, 512], P('quad')
The draws below stay inside these ranges and needn't reach their ends.
Inputs may be any that keep to these rules, and one draw needn't show every extreme that they name: neighbours[c, 0] = c, neighbours[c, 1] = min(c + 2, 319), neighbours[c, 2] = max(c - 2, 0); every entry lies within 2 of c.
All inputs are finite; a program needn't handle non-finite values.
Results may differ from the reference program's by a relative error of at most 0.0075.
Values may be sent and summed in bfloat16 or wider, within the bound.
A program may use at most 64 MiB of HBM per device.

```python
import jax
import jax.numpy as jnp
from jax import lax

ORB = 64
LCOL = 64
QPTS = 32
KMOM = 8
NB = 8
HALO = 2
CELL_DEV = 10
ROWS_Q = 1280
CELLS = 320
ROWS_ALL = 20480
N_QUAD = 16
N_ROWS = 2


def draw_solutions(key, part):
    key = jax.random.fold_in(key, 11)
    first_key, second_key = jax.random.split(key, 2)
    shape = (QPTS, 2, LCOL, N_QUAD, ROWS_Q)
    position = (jnp.arange(N_QUAD, dtype=jnp.int32)[:, None] * ROWS_Q + jnp.arange(ROWS_Q, dtype=jnp.int32)[None, :]).astype(jnp.float32)
    envelope = 0.6 * jnp.exp(jnp.log(3.0) * position / (ROWS_ALL - 1))
    entries = jax.random.truncated_normal(first_key, -4.0, 4.0, shape, jnp.float32)
    factor = jnp.exp(jax.random.uniform(second_key, (N_QUAD, ROWS_Q), jnp.float32, jnp.log(0.5), jnp.log(2.0)))
    share_rows = KMOM * LCOL // N_QUAD
    column = jnp.arange(LCOL, dtype=jnp.int32)
    target = (column // share_rows + N_QUAD // 2) % N_QUAD
    quad_index = jnp.arange(N_QUAD, dtype=jnp.int32)
    row_index = jnp.arange(ROWS_Q, dtype=jnp.int32)
    heavy = (quad_index[None, :, None] == target[:, None, None]) & (row_index[None, None, :] < CELL_DEV * ORB)
    boost = 1.0 + 5.0 * heavy.astype(jnp.float32)
    values = entries * (envelope * factor)[None, None, None, :, :] * boost[None, None, :, :, :]
    values = jnp.clip(values, -60.0, 60.0)
    return values.astype(jnp.bfloat16)


def draw_neighbours(key, part):
    key = jax.random.fold_in(key, 23)
    cell_index = jnp.arange(CELLS, dtype=jnp.int32)[:, None]
    offsets = jax.random.randint(key, (CELLS, NB - 3), -HALO, HALO + 1, dtype=jnp.int32)
    fixed_offsets = jnp.concatenate([jnp.zeros((CELLS, 1), jnp.int32), jnp.full((CELLS, 1), HALO, jnp.int32), jnp.full((CELLS, 1), -HALO, jnp.int32)], 1)
    return jnp.clip(cell_index + jnp.concatenate([fixed_offsets, offsets], 1), 0, CELLS - 1).astype(jnp.int32)


def shard_levels(key, extent, pieces, least, high):
    factor_of = 1.0
    for dim, blocks in pieces:
        draws = jax.random.uniform(jax.random.fold_in(jax.random.fold_in(key, 6), dim), (blocks,), jnp.float32, least / len(pieces), high / len(pieces))
        factor_of = factor_of * jnp.repeat(jnp.exp(draws), extent[dim] // blocks).reshape((-1,) + (1,) * (len(extent) - 1 - dim))
    return factor_of


def noise(key, extent, width, bound, cuts=(), kind=jnp.bfloat16):
    array = jax.random.normal(key, extent, jnp.float32) * width
    if len(cuts) > 0:
        array = shard_levels(key, extent, cuts, -0.22, 0.18) * array
    return jnp.clip(array, min=-bound, max=bound).astype(kind)


def setup_inputs(seed: int = 0) -> dict:
    seeds = jax.random.split(jax.random.key(seed), 6)
    return {
        "solutions": draw_solutions(jax.random.fold_in(seeds[5], 71), 0),
        "angles": jnp.clip(jax.random.uniform(seeds[1], (QPTS,), jnp.float32, -3.140625, 3.140625), -3.140625, 3.140625),
        "qweights": noise(seeds[2], (2, QPTS), QPTS ** -0.5, 1.0, (), jnp.float32),
        "neighbours": draw_neighbours(jax.random.fold_in(seeds[5], 71), 0),
        "hblocks": noise(seeds[4], (CELLS, ORB, NB * ORB), (NB * ORB) ** -0.5, 0.25, ((0, 32),)),
    }


def moment_coefficients(angles, qweights):
    order = jnp.arange(KMOM, dtype=jnp.float32)[:, None]
    phase = order * angles[None, :]
    cosine = jnp.cos(phase)
    sine = jnp.sin(phase)
    real_coef = qweights[0][None, :] * cosine - qweights[1][None, :] * sine
    imag_coef = qweights[0][None, :] * sine + qweights[1][None, :] * cosine
    real_rows = jnp.stack([real_coef, -imag_coef], -1)
    imag_rows = jnp.stack([imag_coef, real_coef], -1)
    mixing = jnp.stack([real_rows, imag_rows], 0)
    return mixing.reshape(2 * KMOM, 2 * QPTS).astype(jnp.bfloat16)


def split_parts(product, half_cols, row_count):
    real_part = product[:row_count, :half_cols] + product[row_count:, half_cols:]
    imag_part = product[:row_count, half_cols:] - product[row_count:, :half_cols]
    return jnp.stack([real_part, imag_part], 1)


def reference(solutions, angles, qweights, neighbours, hblocks):
    mixing = moment_coefficients(angles, qweights).astype(jnp.float32)
    blocks = N_QUAD * N_ROWS
    rows_dev = CELL_DEV * ORB
    half_cols = KMOM * LCOL
    shaped = solutions.reshape(QPTS * 2, LCOL, blocks, rows_dev)

    def moments_of(index):
        segment = lax.dynamic_index_in_dim(shaped, index, 2, keepdims=False).astype(jnp.float32)
        result = jnp.einsum('pq,qln->pln', mixing, segment, precision=lax.Precision.HIGHEST)
        return result.reshape(2 * half_cols, rows_dev).astype(jnp.bfloat16)

    moment_blocks = lax.map(moments_of, jnp.arange(blocks, dtype=jnp.int32))
    cellwise = moment_blocks.transpose(1, 0, 2).reshape(2 * half_cols, CELLS, ORB)
    index_blocks = neighbours.reshape(blocks, CELL_DEV * NB)
    coupling_blocks = hblocks.reshape(blocks, CELL_DEV, ORB, NB * ORB)

    def advance(carry, inputs):
        plain, mixed = carry
        current, indices, couplings = inputs
        nearby = jnp.take(cellwise, indices, axis=1).reshape(2 * half_cols, CELL_DEV, NB * ORB).astype(jnp.float32)
        applied = jnp.einsum('cam,xcm->xca', couplings.astype(jnp.float32), nearby, precision=lax.Precision.HIGHEST)
        applied = applied.reshape(2 * half_cols, rows_dev).astype(jnp.bfloat16)
        plain = plain + jnp.dot(current, current.T, preferred_element_type=jnp.float32)
        mixed = mixed + jnp.dot(current, applied.T, preferred_element_type=jnp.float32)
        return (plain, mixed), applied

    zeros = jnp.zeros((2 * half_cols, 2 * half_cols), jnp.float32)
    (plain, mixed), applied_blocks = lax.scan(advance, (zeros, zeros), (moment_blocks, index_blocks, coupling_blocks))
    h_moments = applied_blocks.transpose(1, 0, 2).reshape(2 * half_cols, CELLS * ORB)
    ritz = jnp.stack([split_parts(plain, half_cols, half_cols), split_parts(mixed, half_cols, half_cols)], 1)
    ritz_matrices = ritz * (1.0 / ROWS_ALL)
    return h_moments, ritz_matrices
```

```python
import jax
import jax.numpy as jnp
from jax import lax
from jax.experimental import pallas as pl
from jax.experimental.pallas import tpu as pltpu
from jax.sharding import PartitionSpec as P

LCOL = 64
QPTS = 32
KMOM = 8
NB = 8
HALO = 2
LC = 16
BOTH = ("quad", "rows")
NT = (((1,), (1,)), ((), ()))


def moment_coefficients(angles, qweights):
    order = jnp.arange(KMOM, dtype=jnp.float32)[:, None]
    phase = order * angles[None, :]
    cosine = jnp.cos(phase)
    sine = jnp.sin(phase)
    real_coef = qweights[0][None, :] * cosine - qweights[1][None, :] * sine
    imag_coef = qweights[0][None, :] * sine + qweights[1][None, :] * cosine
    real_rows = jnp.stack([real_coef, -imag_coef], -1)
    imag_rows = jnp.stack([imag_coef, real_coef], -1)
    mixing = jnp.stack([real_rows, imag_rows], 0)
    return mixing.reshape(2 * KMOM, 2 * QPTS).astype(jnp.bfloat16)


def mixing_kernel(weights, received, moments):
    block = received[...]
    block = block.reshape(block.shape[0] * block.shape[1], block.shape[2])
    result = jnp.dot(weights[...], block, preferred_element_type=jnp.float32)
    moments[...] = result.astype(jnp.bfloat16).reshape(moments.shape)


def mix(wide, received):
    points, columns, rows = received.shape
    parts = 2 * KMOM
    return pl.pallas_call(
        mixing_kernel,
        grid=(columns // LC,),
        out_shape=jax.ShapeDtypeStruct((parts, columns, rows), jnp.bfloat16),
        in_specs=[
            pl.BlockSpec((parts * LC, points * LC), lambda i: (0, 0)),
            pl.BlockSpec((points, LC, rows), lambda i: (0, i, 0)),
        ],
        out_specs=pl.BlockSpec((parts, LC, rows), lambda i: (0, i, 0)),
        compiler_params=pltpu.CompilerParams(vmem_limit_bytes=32 * 2**20),
    )(wide, received)


def gram_kernel(low, moments, high, band, applied, gram):
    pairs, width, reach = band.shape
    rows = moments.shape[1]
    side = low.shape[1]
    half = moments.shape[0] // 2
    padded = jnp.concatenate([low[...], moments[...], high[...]], 1)
    for i in range(pairs):
        out = lax.dot_general(
            padded[:, i * width : i * width + reach], band[i], NT, preferred_element_type=jnp.float32
        )
        applied[:, i * width : (i + 1) * width] = out.astype(jnp.bfloat16)

    def prod(left, right):
        return lax.dot_general(left, right, NT, preferred_element_type=jnp.float32)

    real, imag = moments[:half, :], moments[half:, :]
    for m, right in enumerate((moments, applied)):
        other_real, other_imag = right[:half, :], right[half:, :]
        gram[:, (2 * m) * half : (2 * m + 1) * half] = prod(real, other_real) + prod(imag, other_imag)
        gram[:, (2 * m + 1) * half : (2 * m + 2) * half] = prod(real, other_imag) - prod(imag, other_real)


def apply_and_gram(low, moments, high, band):
    total, rows = moments.shape
    half = total // 2
    return pl.pallas_call(
        gram_kernel,
        out_shape=(
            jax.ShapeDtypeStruct((total, rows), jnp.bfloat16),
            jax.ShapeDtypeStruct((half, 4 * half), jnp.float32),
        ),
        in_specs=[pl.BlockSpec(memory_space=pltpu.VMEM)] * 4,
        out_specs=(pl.BlockSpec(memory_space=pltpu.VMEM),) * 2,
        compiler_params=pltpu.CompilerParams(vmem_limit_bytes=40 * 2**20),
    )(low, moments, high, band)


def band_blocks(neighbours, hblocks, first_cell):
    cells, orbitals, _ = hblocks.shape
    pairs = cells // 2
    window = 2 * HALO + 2
    local = (neighbours - first_cell + HALO).reshape(pairs, 2, NB) - 2 * jnp.arange(pairs)[:, None, None]
    split = hblocks.reshape(pairs, 2, orbitals, NB * orbitals)
    chosen = []
    for d in range(window):
        total = 0.0
        for n in range(NB):
            hit = (local[:, :, n] == d).astype(jnp.float32)[:, :, None, None]
            total += hit * split[:, :, :, n * orbitals : (n + 1) * orbitals].astype(jnp.float32)
        chosen.append(total.astype(jnp.bfloat16))
    return jnp.concatenate(chosen, -1).reshape(pairs, 2 * orbitals, window * orbitals)


def butterfly(gram, quads, rows):
    share = gram.shape[0] // quads
    me = lax.axis_index("quad")
    part = gram.reshape(quads, share, gram.shape[1])
    step = 1
    while step < quads:
        bit = (me // step) % 2
        split = part.reshape(part.shape[0] // 2, 2, share, part.shape[2])
        mine = lax.dynamic_index_in_dim(split, bit, 1, keepdims=False)
        other = lax.dynamic_index_in_dim(split, 1 - bit, 1, keepdims=False).astype(jnp.bfloat16)
        got = lax.ppermute(other, "quad", [(i, i ^ step) for i in range(quads)])
        part = mine + got.astype(jnp.float32)
        step *= 2
    part = part.reshape(share, gram.shape[1])
    step = 1
    while step < rows:
        part = part + lax.ppermute(part, "rows", [(i, i ^ step) for i in range(rows)])
        step *= 2
    return part


def per_device(solutions, angles, qweights, neighbours, hblocks):
    quads, rows = lax.axis_size("quad"), lax.axis_size("rows")
    groups = quads * rows
    rows_dev = solutions.shape[4]
    cells_dev = hblocks.shape[0]
    orbitals = hblocks.shape[1]
    half_cols = KMOM * LCOL
    mixing = moment_coefficients(angles, qweights)
    wide = (
        mixing[:, None, :, None] * jnp.eye(LC, dtype=jnp.bfloat16)[None, :, None, :]
    ).reshape(2 * KMOM * LC, 2 * QPTS * LC)
    first_cell = (lax.axis_index("quad") * rows + lax.axis_index("rows")) * cells_dev
    band = band_blocks(neighbours, hblocks, first_cell)
    received = lax.all_to_all(solutions, "quad", split_axis=3, concat_axis=0, tiled=True)
    stacked = received.reshape(QPTS * 2, LCOL, rows_dev)
    moments = mix(wide, stacked).reshape(2 * half_cols, rows_dev)
    side = HALO * orbitals
    forward = [(i, i + 1) for i in range(groups - 1)]
    backward = [(i + 1, i) for i in range(groups - 1)]
    low = lax.ppermute(moments[:, rows_dev - side :], BOTH, forward)
    high = lax.ppermute(moments[:, :side], BOTH, backward)
    applied, gram = apply_and_gram(low, moments, high, band)
    ritz = butterfly(gram, quads, rows) * (1.0 / (rows_dev * groups))
    return applied, ritz.reshape(half_cols // quads, 2, 2, half_cols)


def solution(mesh):
    in_specs = (
        P("quad", None, None, None, "rows"),
        P(),
        P(),
        P(BOTH, None),
        P(BOTH, None, None),
    )
    out_specs = (P(None, BOTH), P("quad", None, None, None))
    return jax.shard_map(
        per_device, mesh=mesh, in_specs=in_specs, out_specs=out_specs, check_vma=False
    )
```

```python
import functools

import jax
import jax.numpy as jnp
from jax import lax
from jax.experimental import pallas as pl
from jax.experimental.pallas import tpu as pltpu
from jax.sharding import PartitionSpec as P

LCOL = 64
QPTS = 32
KMOM = 8
NB = 8
HALO = 2
LC = 16
BOTH = ("quad", "rows")
NT = (((1,), (1,)), ((), ()))
MESH = pl.DeviceIdType.MESH


def moment_coefficients(angles, qweights):
    order = jnp.arange(KMOM, dtype=jnp.float32)[:, None]
    phase = order * angles[None, :]
    cosine = jnp.cos(phase)
    sine = jnp.sin(phase)
    real_coef = qweights[0][None, :] * cosine - qweights[1][None, :] * sine
    imag_coef = qweights[0][None, :] * sine + qweights[1][None, :] * cosine
    real_rows = jnp.stack([real_coef, -imag_coef], -1)
    imag_rows = jnp.stack([imag_coef, real_coef], -1)
    mixing = jnp.stack([real_rows, imag_rows], 0)
    return mixing.reshape(2 * KMOM, 2 * QPTS).astype(jnp.bfloat16)


def step_plan(quads):
    bits = quads.bit_length() - 1
    rising = [(1 << i, True) for i in range(bits)]
    falling = [(1, True)] + [(1 << i, False) for i in range(bits - 1, 0, -1)]
    return rising, falling


def fused_kernel(
    quads, groups_r, scale, solutions, mixing, band, applied, ritz,
    outgoing, incoming, moments, low, high, wide, gram, sent, got, last, last_got,
    own_sem, a2a_send, a2a_recv, halo_send, halo_recv, step_send, step_recv, row_send, row_recv,
):
    points, columns, owners, rows = solutions.shape
    chunks = columns // LC
    parts = 2 * KMOM
    half = KMOM * columns
    share = half // quads
    pairs, width, reach = band.shape
    side = low.shape[-1]
    me = lax.axis_index("quad")
    row = lax.axis_index("rows")
    flat = me * groups_r + row
    total = quads * groups_r
    after, before = lax.rem(flat + 1, total), lax.rem(flat + total - 1, total)
    after = {"quad": after // groups_r, "rows": lax.rem(after, groups_r)}
    before = {"quad": before // groups_r, "rows": lax.rem(before, groups_r)}
    row_steps = [1 << i for i in range(groups_r.bit_length() - 1)]

    def partner(index, step):
        return index + step - 2 * step * lax.rem(index // step, 2)

    def copy_out(c, o):
        target = lax.rem(me + o, quads)
        return pltpu.make_async_remote_copy(
            src_ref=outgoing.at[c, target],
            dst_ref=incoming.at[c, pl.ds(me * points, points)],
            send_sem=a2a_send.at[c, o],
            recv_sem=a2a_recv.at[c, o],
            device_id={"quad": target},
            device_id_type=MESH,
        )

    def own_copy(c):
        return pltpu.make_async_copy(
            outgoing.at[c, me], incoming.at[c, pl.ds(me * points, points)], own_sem.at[c]
        )

    size = owners * LC
    r_index = lax.broadcasted_iota(jnp.int32, (size, size), 0)
    c_index = lax.broadcasted_iota(jnp.int32, (size, size), 1)
    swap = jnp.where(
        (r_index // LC == lax.rem(c_index, owners)) & (lax.rem(r_index, LC) == c_index // owners), 1.0, 0.0
    ).astype(jnp.bfloat16)

    def rearrange(c):
        def one(q, carry):
            block = solutions[q, c * LC : (c + 1) * LC].reshape(size, rows)
            moved = jnp.dot(swap, block, preferred_element_type=jnp.float32).astype(jnp.bfloat16)
            outgoing[c, :, q] = moved.reshape(owners, LC, rows)
            return carry

        lax.fori_loop(0, points, one, 0)

    barrier = pltpu.get_barrier_semaphore()

    def greet(o, carry):
        pl.semaphore_signal(
            barrier, inc=1, device_id={"quad": lax.rem(me + o, quads)}, device_id_type=MESH
        )
        return carry

    lax.fori_loop(1, quads, greet, 0)
    pl.semaphore_signal(barrier, inc=1, device_id=after, device_id_type=MESH)
    pl.semaphore_signal(barrier, inc=1, device_id=before, device_id_type=MESH)
    for step in row_steps:
        pl.semaphore_signal(
            barrier, inc=1, device_id={"rows": partner(row, step)}, device_id_type=MESH
        )
    rearrange(0)
    pl.semaphore_wait(barrier, quads + 1 + len(row_steps))

    for c in range(chunks):
        if c:
            rearrange(c)

        def send(o, carry):
            copy_out(c, o).start()
            return carry

        lax.fori_loop(1, quads, send, 0)
        own_copy(c).start()

    high_rows, deep = wide.shape
    spread_p = jnp.where(
        lax.broadcasted_iota(jnp.int32, (high_rows, parts), 0) // LC
        == lax.broadcasted_iota(jnp.int32, (high_rows, parts), 1), 1.0, 0.0,
    ).astype(jnp.bfloat16)
    spread_q = jnp.where(
        lax.broadcasted_iota(jnp.int32, (deep // LC, deep), 1) // LC
        == lax.broadcasted_iota(jnp.int32, (deep // LC, deep), 0), 1.0, 0.0,
    ).astype(jnp.bfloat16)
    tall = jnp.dot(spread_p, mixing[...], preferred_element_type=jnp.float32).astype(jnp.bfloat16)
    full = jnp.dot(tall, spread_q, preferred_element_type=jnp.float32)
    same = lax.rem(lax.broadcasted_iota(jnp.int32, (high_rows, deep), 0), LC) == lax.rem(
        lax.broadcasted_iota(jnp.int32, (high_rows, deep), 1), LC
    )
    wide[...] = jnp.where(same, full, 0.0).astype(jnp.bfloat16)

    def halo_copies(c):
        up = pltpu.make_async_remote_copy(
            src_ref=moments.at[:, c, :, rows - side : rows],
            dst_ref=low.at[:, c],
            send_sem=halo_send.at[0, c],
            recv_sem=halo_recv.at[0, c],
            device_id=after,
            device_id_type=MESH,
        )
        down = pltpu.make_async_remote_copy(
            src_ref=moments.at[:, c, :, 0:side],
            dst_ref=high.at[:, c],
            send_sem=halo_send.at[1, c],
            recv_sem=halo_recv.at[1, c],
            device_id=before,
            device_id_type=MESH,
        )
        return up, down

    def apply_band(c):
        for copy in halo_copies(c):
            copy.wait_recv()
        near = jnp.concatenate([low[:, c], moments[:, c], high[:, c]], -1)
        near = near.reshape(parts * LC, rows + 2 * side)
        for i in range(pairs):
            out = lax.dot_general(
                near[:, i * width : i * width + reach], band[i], NT, preferred_element_type=jnp.float32
            )
            applied[:, c, :, i * width : (i + 1) * width] = out.astype(jnp.bfloat16).reshape(
                parts, LC, width
            )

    for c in range(chunks):
        own_copy(c).wait()

        def arrive(o, carry):
            copy_out(c, o).wait_recv()
            return carry

        lax.fori_loop(1, quads, arrive, 0)
        block = incoming[c].reshape(deep, rows)
        mixed = jnp.dot(wide[...], block, preferred_element_type=jnp.float32)
        moments[:, c] = mixed.astype(jnp.bfloat16).reshape(parts, LC, rows)
        for copy in halo_copies(c):
            copy.start()
        if c:
            apply_band(c - 1)

    def prod(left, right):
        return lax.dot_general(left, right, NT, preferred_element_type=jnp.float32)

    def grams(m, right):
        real = moments[:KMOM].reshape(half, rows)
        imag = moments[KMOM:].reshape(half, rows)
        other_real = right[:KMOM].reshape(half, rows)
        other_imag = right[KMOM:].reshape(half, rows)
        plain = prod(real, other_real) + prod(imag, other_imag)
        gram[m, :, :, :half] = plain.reshape(quads, share, half)
        cross = prod(real, other_imag) - prod(imag, other_real)
        gram[m, :, :, half:] = cross.reshape(quads, share, half)

    plans = step_plan(quads)
    steps = len(plans[0])

    def place(s):
        return quads - (quads >> s)

    def step_copy(m, s):
        bit, _ = plans[m][s]
        count = quads >> (s + 1)
        return pltpu.make_async_remote_copy(
            src_ref=sent.at[m, pl.ds(place(s), count)],
            dst_ref=got.at[m, pl.ds(place(s), count)],
            send_sem=step_send.at[m, s],
            recv_sem=step_recv.at[m, s],
            device_id={"quad": partner(me, bit)},
            device_id_type=MESH,
        )

    def position(m, s, j, side_bit):
        _, rising = plans[m][s]
        count = quads >> (s + 1)
        return 2 * j + side_bit if rising else j + side_bit * count

    def pack(m, s):
        bit, _ = plans[m][s]
        mine = lax.rem(me // bit, 2)

        def one(j, carry):
            sent[m, place(s) + j] = gram[m, position(m, s, j, 1 - mine)].astype(jnp.bfloat16)
            return carry

        lax.fori_loop(0, quads >> (s + 1), one, 0)
        step_copy(m, s).start()

    def gather(m, s):
        bit, _ = plans[m][s]
        mine = lax.rem(me // bit, 2)
        step_copy(m, s).wait_recv()

        def one(j, carry):
            gram[m, j] = gram[m, position(m, s, j, mine)] + got[m, place(s) + j].astype(jnp.float32)
            return carry

        lax.fori_loop(0, quads >> (s + 1), one, 0)

    def row_copy(m, s):
        return pltpu.make_async_remote_copy(
            src_ref=last.at[m, s],
            dst_ref=last_got.at[m, s],
            send_sem=row_send.at[m, s],
            recv_sem=row_recv.at[m, s],
            device_id={"rows": partner(row, row_steps[s])},
            device_id_type=MESH,
        )

    grams(0, moments)
    pack(0, 0)
    apply_band(chunks - 1)
    grams(1, applied)
    pack(1, 0)
    for s in range(steps):
        for m in range(2):
            gather(m, s)
            if s + 1 < steps:
                pack(m, s + 1)
            else:
                last[m, 0] = gram[m, 0]
                row_copy(m, 0).start()
    for s in range(len(row_steps)):
        for m in range(2):
            row_copy(m, s).wait_recv()
            summed = last[m, s] + last_got[m, s]
            if s + 1 < len(row_steps):
                last[m, s + 1] = summed
                row_copy(m, s + 1).start()
            else:
                ritz[:, 2 * m * half : 2 * (m + 1) * half] = summed * scale

    for c in range(chunks):

        def leave(o, carry):
            copy_out(c, o).wait_send()
            return carry

        lax.fori_loop(1, quads, leave, 0)
        for copy in halo_copies(c):
            copy.wait_send()
    for m in range(2):
        for s in range(steps):
            step_copy(m, s).wait_send()
        for s in range(len(row_steps)):
            row_copy(m, s).wait_send()


def fused(solutions, mixing, band, quads, groups_r, scale):
    points, columns, owners, rows = solutions.shape
    chunks = columns // LC
    parts = 2 * KMOM
    half = KMOM * columns
    share = half // quads
    side = (band.shape[2] - band.shape[1]) // 2
    steps = quads.bit_length() - 1
    row_steps = groups_r.bit_length() - 1
    bf, f4 = jnp.bfloat16, jnp.float32
    dma = pltpu.SemaphoreType.DMA
    return pl.pallas_call(
        functools.partial(fused_kernel, quads, groups_r, scale),
        out_shape=(
            jax.ShapeDtypeStruct((parts, chunks, LC, rows), bf),
            jax.ShapeDtypeStruct((share, 4 * half), f4),
        ),
        in_specs=[pl.BlockSpec(memory_space=pltpu.VMEM)] * 3,
        out_specs=(pl.BlockSpec(memory_space=pltpu.VMEM),) * 2,
        scratch_shapes=[
            pltpu.VMEM((chunks, owners, points, LC, rows), bf),
            pltpu.VMEM((chunks, owners * points, LC, rows), bf),
            pltpu.VMEM((parts, chunks, LC, rows), bf),
            pltpu.VMEM((parts, chunks, LC, side), bf),
            pltpu.VMEM((parts, chunks, LC, side), bf),
            pltpu.VMEM((parts * LC, owners * points * LC), bf),
            pltpu.VMEM((2, quads, share, 2 * half), f4),
            pltpu.VMEM((2, quads, share, 2 * half), bf),
            pltpu.VMEM((2, quads, share, 2 * half), bf),
            pltpu.VMEM((2, row_steps, share, 2 * half), f4),
            pltpu.VMEM((2, row_steps, share, 2 * half), f4),
            dma((chunks,)),
            dma((chunks, quads)),
            dma((chunks, quads)),
            dma((2, chunks)),
            dma((2, chunks)),
            dma((2, steps)),
            dma((2, steps)),
            dma((2, row_steps)),
            dma((2, row_steps)),
        ],
        compiler_params=pltpu.CompilerParams(
            collective_id=0, has_side_effects=True, vmem_limit_bytes=56 * 2**20
        ),
    )(solutions, mixing, band)


def band_blocks(neighbours, hblocks, first_cell):
    cells, orbitals, _ = hblocks.shape
    pairs = cells // 2
    window = 2 * HALO + 2
    local = (neighbours - first_cell + HALO).reshape(pairs, 2, NB) - 2 * jnp.arange(pairs)[:, None, None]
    split = hblocks.reshape(pairs, 2, orbitals, NB * orbitals)
    chosen = []
    for d in range(window):
        total = 0.0
        for n in range(NB):
            hit = (local[:, :, n] == d).astype(jnp.float32)[:, :, None, None]
            total += hit * split[:, :, :, n * orbitals : (n + 1) * orbitals].astype(jnp.float32)
        chosen.append(total.astype(jnp.bfloat16))
    return jnp.concatenate(chosen, -1).reshape(pairs, 2 * orbitals, window * orbitals)


def per_device(solutions, angles, qweights, neighbours, hblocks):
    quads, rows = lax.axis_size("quad"), lax.axis_size("rows")
    rows_dev = solutions.shape[4]
    cells_dev = hblocks.shape[0]
    half_cols = KMOM * LCOL
    mixing = moment_coefficients(angles, qweights)
    first_cell = (lax.axis_index("quad") * rows + lax.axis_index("rows")) * cells_dev
    band = band_blocks(neighbours, hblocks, first_cell)
    shaped = solutions.reshape((-1,) + solutions.shape[2:])
    applied, ritz = fused(shaped, mixing, band, quads, rows, 1.0 / (rows_dev * quads * rows))
    return (
        applied.reshape(2 * half_cols, rows_dev),
        ritz.reshape(half_cols // quads, 2, 2, half_cols),
    )


def solution(mesh):
    in_specs = (
        P("quad", None, None, None, "rows"),
        P(),
        P(),
        P(BOTH, None),
        P(BOTH, None, None),
    )
    out_specs = (P(None, BOTH), P("quad", None, None, None))
    return jax.shard_map(
        per_device, mesh=mesh, in_specs=in_specs, out_specs=out_specs, check_vma=False
    )
```

```python
import functools

import jax
import jax.numpy as jnp
from jax import lax
from jax.experimental import pallas as pl
from jax.experimental.pallas import tpu as pltpu
from jax.sharding import PartitionSpec as P

LCOL = 64
QPTS = 32
KMOM = 8
NB = 8
HALO = 2
LC = 16
LINE = 4
BOTH = ("quad", "rows")
NT = (((1,), (1,)), ((), ()))
MESH = pl.DeviceIdType.MESH


def moment_coefficients(angles, qweights):
    order = jnp.arange(KMOM, dtype=jnp.float32)[:, None]
    phase = order * angles[None, :]
    cosine = jnp.cos(phase)
    sine = jnp.sin(phase)
    real_coef = qweights[0][None, :] * cosine - qweights[1][None, :] * sine
    imag_coef = qweights[0][None, :] * sine + qweights[1][None, :] * cosine
    real_rows = jnp.stack([real_coef, -imag_coef], -1)
    imag_rows = jnp.stack([imag_coef, real_coef], -1)
    mixing = jnp.stack([real_rows, imag_rows], 0)
    return mixing.reshape(2 * KMOM, 2 * QPTS).astype(jnp.bfloat16)


def step_plan(quads):
    bits = quads.bit_length() - 1
    rising = [(1 << i, True) for i in range(bits)]
    falling = [(1, True)] + [(1 << i, False) for i in range(bits - 1, 0, -1)]
    return rising, falling


def fused_kernel(
    quads, groups_r, scale, solutions, mixing, band, applied, ritz,
    outgoing, incoming, passed, landed, moments, low, high, wide, gram, sent, got, last, last_got,
    own_sem, a2a_send, a2a_recv, line_send, line_recv, halo_send, halo_recv, step_send, step_recv, row_send, row_recv,
):
    points, columns, owners, rows = solutions.shape
    chunks = columns // LC
    parts = 2 * KMOM
    half = KMOM * columns
    share = half // quads
    pairs, width, reach = band.shape
    side = low.shape[-1]
    me = lax.axis_index("quad")
    row = lax.axis_index("rows")
    flat = me * groups_r + row
    total = quads * groups_r
    after, before = lax.rem(flat + 1, total), lax.rem(flat + total - 1, total)
    after = {"quad": after // groups_r, "rows": lax.rem(after, groups_r)}
    before = {"quad": before // groups_r, "rows": lax.rem(before, groups_r)}
    row_steps = [1 << i for i in range(groups_r.bit_length() - 1)]

    def partner(index, step):
        return index + step - 2 * step * lax.rem(index // step, 2)

    group = quads // LINE
    spot = lax.rem(me, group)
    line = me // group

    def copy_out(c, o):
        target = lax.rem(spot + o, group)
        return pltpu.make_async_remote_copy(
            src_ref=outgoing.at[c, target],
            dst_ref=incoming.at[c, spot],
            send_sem=a2a_send.at[c, o],
            recv_sem=a2a_recv.at[c, o],
            device_id={"quad": line * group + target},
            device_id_type=MESH,
        )

    def own_copy(c):
        return pltpu.make_async_copy(outgoing.at[c, spot], incoming.at[c, spot], own_sem.at[c])

    def line_copy(c, slot, landing, shift):
        return pltpu.make_async_remote_copy(
            src_ref=passed.at[c, slot],
            dst_ref=landed.at[c, landing],
            send_sem=line_send.at[c, slot],
            recv_sem=line_recv.at[c, landing],
            device_id={"quad": lax.rem(me + shift + quads, quads)},
            device_id_type=MESH,
        )

    size = owners * LC
    r_index = lax.broadcasted_iota(jnp.int32, (size, size), 0)
    c_index = lax.broadcasted_iota(jnp.int32, (size, size), 1)
    swap = jnp.where(
        (lax.rem(r_index // LC, LINE) * group + r_index // (LC * LINE) == lax.rem(c_index, owners)) & (lax.rem(r_index, LC) == c_index // owners), 1.0, 0.0
    ).astype(jnp.bfloat16)

    def rearrange(c):
        def one(q, carry):
            block = solutions[q, c * LC : (c + 1) * LC].reshape(size, rows)
            moved = jnp.dot(swap, block, preferred_element_type=jnp.float32).astype(jnp.bfloat16)
            outgoing[c, :, :, q] = moved.reshape(group, LINE, LC, rows)
            return carry

        lax.fori_loop(0, points, one, 0)

    barrier = pltpu.get_barrier_semaphore()

    near_by = [line * group + lax.rem(spot + o, group) for o in range(1, group)]
    near_by += [lax.rem(me + group, quads), lax.rem(me + quads - group, quads)]
    near_by += [partner(me, 1 << b) for b in range(quads.bit_length() - 1)]
    for other in near_by:
        pl.semaphore_signal(barrier, inc=1, device_id={"quad": other}, device_id_type=MESH)
    pl.semaphore_signal(barrier, inc=1, device_id=after, device_id_type=MESH)
    pl.semaphore_signal(barrier, inc=1, device_id=before, device_id_type=MESH)
    for step in row_steps:
        pl.semaphore_signal(
            barrier, inc=1, device_id={"rows": partner(row, step)}, device_id_type=MESH
        )
    rearrange(0)
    pl.semaphore_wait(barrier, len(near_by) + 2 + len(row_steps))

    for c in range(chunks):
        if c:
            rearrange(c)

        def send(o, carry):
            copy_out(c, o).start()
            return carry

        lax.fori_loop(1, group, send, 0)
        own_copy(c).start()

    high_rows, deep = wide.shape
    spread_p = jnp.where(
        lax.broadcasted_iota(jnp.int32, (high_rows, parts), 0) // LC
        == lax.broadcasted_iota(jnp.int32, (high_rows, parts), 1), 1.0, 0.0,
    ).astype(jnp.bfloat16)
    all_points = mixing.shape[1]
    spread_q = jnp.where(
        lax.broadcasted_iota(jnp.int32, (all_points, deep), 1) // LC + line * (deep // LC)
        == lax.broadcasted_iota(jnp.int32, (all_points, deep), 0), 1.0, 0.0,
    ).astype(jnp.bfloat16)
    tall = jnp.dot(spread_p, mixing[...], preferred_element_type=jnp.float32).astype(jnp.bfloat16)
    full = jnp.dot(tall, spread_q, preferred_element_type=jnp.float32)
    same = lax.rem(lax.broadcasted_iota(jnp.int32, (high_rows, deep), 0), LC) == lax.rem(
        lax.broadcasted_iota(jnp.int32, (high_rows, deep), 1), LC
    )
    wide[...] = jnp.where(same, full, 0.0).astype(jnp.bfloat16)

    def halo_copies(c):
        up = pltpu.make_async_remote_copy(
            src_ref=moments.at[:, c, :, rows - side : rows],
            dst_ref=low.at[:, c],
            send_sem=halo_send.at[0, c],
            recv_sem=halo_recv.at[0, c],
            device_id=after,
            device_id_type=MESH,
        )
        down = pltpu.make_async_remote_copy(
            src_ref=moments.at[:, c, :, 0:side],
            dst_ref=high.at[:, c],
            send_sem=halo_send.at[1, c],
            recv_sem=halo_recv.at[1, c],
            device_id=before,
            device_id_type=MESH,
        )
        return up, down

    def apply_band(c):
        for copy in halo_copies(c):
            copy.wait_recv()
        near = jnp.concatenate([low[:, c], moments[:, c], high[:, c]], -1)
        near = near.reshape(parts * LC, rows + 2 * side)
        for i in range(pairs):
            out = lax.dot_general(
                near[:, i * width : i * width + reach], band[i], NT, preferred_element_type=jnp.float32
            )
            applied[:, c, :, i * width : (i + 1) * width] = out.astype(jnp.bfloat16).reshape(
                parts, LC, width
            )

    def partial_sum(c, slot):
        block = incoming[c, :, slot].reshape(deep, rows)
        return jnp.dot(wide[...], block, preferred_element_type=jnp.float32).reshape(parts, LC, rows)

    def forward(c):
        for slot in list(range(LINE - 1, 0, -1)):

            @pl.when((line == 0) & (slot > 0))
            def _():
                passed[c, slot] = partial_sum(c, slot).astype(jnp.bfloat16)
                line_copy(c, slot, slot, group).start()

            @pl.when((line > 0) & (line < slot))
            def _():
                value = partial_sum(c, slot)
                line_copy(c, slot, slot, group).wait_recv()
                passed[c, slot] = (value + landed[c, slot].astype(jnp.float32)).astype(jnp.bfloat16)
                line_copy(c, slot, slot, group).start()

        for slot in range(LINE - 1):

            @pl.when(line > slot)
            def _():
                value = partial_sum(c, slot)

                @pl.when(line == LINE - 1)
                def _():
                    passed[c, slot] = value.astype(jnp.bfloat16)

                @pl.when(line < LINE - 1)
                def _():
                    line_copy(c, slot, slot, -group).wait_recv()
                    passed[c, slot] = (value + landed[c, slot].astype(jnp.float32)).astype(jnp.bfloat16)

                landing = jnp.where(line - 1 == slot, LINE, slot)
                line_copy(c, slot, landing, -group).start()

    def finish(c):
        base = partial_sum(c, line)

        @pl.when(line == 0)
        def _():
            line_copy(c, 0, LINE, -group).wait_recv()
            moments[:, c] = (base + landed[c, LINE].astype(jnp.float32)).astype(jnp.bfloat16)

        @pl.when(line == LINE - 1)
        def _():
            line_copy(c, 0, LINE - 1, group).wait_recv()
            moments[:, c] = (base + landed[c, LINE - 1].astype(jnp.float32)).astype(jnp.bfloat16)

        @pl.when((line > 0) & (line < LINE - 1))
        def _():
            line_copy(c, 0, line, group).wait_recv()
            line_copy(c, 0, LINE, -group).wait_recv()
            both = landed[c, line].astype(jnp.float32) + landed[c, LINE].astype(jnp.float32)
            moments[:, c] = (base + both).astype(jnp.bfloat16)

        for copy in halo_copies(c):
            copy.start()

    for c in range(chunks):
        own_copy(c).wait()

        def arrive(o, carry):
            copy_out(c, o).wait_recv()
            return carry

        lax.fori_loop(1, group, arrive, 0)
        forward(c)
        if c:
            finish(c - 1)
        if c > 1:
            apply_band(c - 2)
    finish(chunks - 1)
    apply_band(chunks - 2)

    def prod(left, right):
        return lax.dot_general(left, right, NT, preferred_element_type=jnp.float32)

    def grams(m, right):
        real = moments[:KMOM].reshape(half, rows)
        imag = moments[KMOM:].reshape(half, rows)
        other_real = right[:KMOM].reshape(half, rows)
        other_imag = right[KMOM:].reshape(half, rows)
        plain = prod(real, other_real) + prod(imag, other_imag)
        gram[m, :, :, :half] = plain.reshape(quads, share, half)
        cross = prod(real, other_imag) - prod(imag, other_real)
        gram[m, :, :, half:] = cross.reshape(quads, share, half)

    plans = step_plan(quads)
    steps = len(plans[0])

    def place(s):
        return quads - (quads >> s)

    def step_copy(m, s):
        bit, _ = plans[m][s]
        count = quads >> (s + 1)
        return pltpu.make_async_remote_copy(
            src_ref=sent.at[m, pl.ds(place(s), count)],
            dst_ref=got.at[m, pl.ds(place(s), count)],
            send_sem=step_send.at[m, s],
            recv_sem=step_recv.at[m, s],
            device_id={"quad": partner(me, bit)},
            device_id_type=MESH,
        )

    def position(m, s, j, side_bit):
        _, rising = plans[m][s]
        count = quads >> (s + 1)
        return 2 * j + side_bit if rising else j + side_bit * count

    def pack(m, s):
        bit, _ = plans[m][s]
        mine = lax.rem(me // bit, 2)

        def one(j, carry):
            sent[m, place(s) + j] = gram[m, position(m, s, j, 1 - mine)].astype(jnp.bfloat16)
            return carry

        lax.fori_loop(0, quads >> (s + 1), one, 0)
        step_copy(m, s).start()

    def gather(m, s):
        bit, _ = plans[m][s]
        mine = lax.rem(me // bit, 2)
        step_copy(m, s).wait_recv()

        def one(j, carry):
            gram[m, j] = gram[m, position(m, s, j, mine)] + got[m, place(s) + j].astype(jnp.float32)
            return carry

        lax.fori_loop(0, quads >> (s + 1), one, 0)

    def row_copy(m, s):
        return pltpu.make_async_remote_copy(
            src_ref=last.at[m, s],
            dst_ref=last_got.at[m, s],
            send_sem=row_send.at[m, s],
            recv_sem=row_recv.at[m, s],
            device_id={"rows": partner(row, row_steps[s])},
            device_id_type=MESH,
        )

    grams(0, moments)
    pack(0, 0)
    apply_band(chunks - 1)
    grams(1, applied)
    pack(1, 0)
    for s in range(steps):
        for m in range(2):
            gather(m, s)
            if s + 1 < steps:
                pack(m, s + 1)
            else:
                last[m, 0] = gram[m, 0]
                row_copy(m, 0).start()
    for s in range(len(row_steps)):
        for m in range(2):
            row_copy(m, s).wait_recv()
            summed = last[m, s] + last_got[m, s]
            if s + 1 < len(row_steps):
                last[m, s + 1] = summed
                row_copy(m, s + 1).start()
            else:
                for p in range(2):
                    ritz[:, m, p, :] = summed[:, p * half : (p + 1) * half] * scale

    for c in range(chunks):

        def leave(o, carry):
            copy_out(c, o).wait_send()
            return carry

        lax.fori_loop(1, group, leave, 0)
        for copy in halo_copies(c):
            copy.wait_send()
        for slot in range(LINE):

            @pl.when(line != slot)
            def _():
                line_copy(c, slot, slot, group).wait_send()

    for m in range(2):
        for s in range(steps):
            step_copy(m, s).wait_send()
        for s in range(len(row_steps)):
            row_copy(m, s).wait_send()


def fused(solutions, mixing, band, quads, groups_r, scale):
    points, columns, owners, rows = solutions.shape
    chunks = columns // LC
    parts = 2 * KMOM
    half = KMOM * columns
    share = half // quads
    side = (band.shape[2] - band.shape[1]) // 2
    group = quads // LINE
    steps = quads.bit_length() - 1
    row_steps = groups_r.bit_length() - 1
    bf, f4 = jnp.bfloat16, jnp.float32
    dma = pltpu.SemaphoreType.DMA
    return pl.pallas_call(
        functools.partial(fused_kernel, quads, groups_r, scale),
        out_shape=(
            jax.ShapeDtypeStruct((parts, chunks, LC, rows), bf),
            jax.ShapeDtypeStruct((share, 2, 2, half), f4),
        ),
        in_specs=[pl.BlockSpec(memory_space=pltpu.VMEM)] * 3,
        out_specs=(pl.BlockSpec(memory_space=pltpu.VMEM),) * 2,
        scratch_shapes=[
            pltpu.VMEM((chunks, group, LINE, points, LC, rows), bf),
            pltpu.VMEM((chunks, group, LINE, points, LC, rows), bf),
            pltpu.VMEM((chunks, LINE, parts, LC, rows), bf),
            pltpu.VMEM((chunks, LINE + 1, parts, LC, rows), bf),
            pltpu.VMEM((parts, chunks, LC, rows), bf),
            pltpu.VMEM((parts, chunks, LC, side), bf),
            pltpu.VMEM((parts, chunks, LC, side), bf),
            pltpu.VMEM((parts * LC, group * points * LC), bf),
            pltpu.VMEM((2, quads, share, 2 * half), f4),
            pltpu.VMEM((2, quads, share, 2 * half), bf),
            pltpu.VMEM((2, quads, share, 2 * half), bf),
            pltpu.VMEM((2, row_steps, share, 2 * half), f4),
            pltpu.VMEM((2, row_steps, share, 2 * half), f4),
            dma((chunks,)),
            dma((chunks, group)),
            dma((chunks, group)),
            dma((chunks, LINE)),
            dma((chunks, LINE + 1)),
            dma((2, chunks)),
            dma((2, chunks)),
            dma((2, steps)),
            dma((2, steps)),
            dma((2, row_steps)),
            dma((2, row_steps)),
        ],
        compiler_params=pltpu.CompilerParams(
            collective_id=0, has_side_effects=True, vmem_limit_bytes=56 * 2**20
        ),
    )(solutions, mixing, band)


def band_blocks(neighbours, hblocks, first_cell):
    cells, orbitals, _ = hblocks.shape
    pairs = cells // 2
    window = 2 * HALO + 2
    local = (neighbours - first_cell + HALO).reshape(pairs, 2, NB) - 2 * jnp.arange(pairs)[:, None, None]
    split = hblocks.reshape(pairs, 2, orbitals, NB * orbitals)
    chosen = []
    for d in range(window):
        total = 0.0
        for n in range(NB):
            hit = (local[:, :, n] == d).astype(jnp.float32)[:, :, None, None]
            total += hit * split[:, :, :, n * orbitals : (n + 1) * orbitals].astype(jnp.float32)
        chosen.append(total.astype(jnp.bfloat16))
    return jnp.concatenate(chosen, -1).reshape(pairs, 2 * orbitals, window * orbitals)


def per_device(solutions, angles, qweights, neighbours, hblocks):
    quads, rows = lax.axis_size("quad"), lax.axis_size("rows")
    rows_dev = solutions.shape[4]
    cells_dev = hblocks.shape[0]
    half_cols = KMOM * LCOL
    mixing = moment_coefficients(angles, qweights)
    first_cell = (lax.axis_index("quad") * rows + lax.axis_index("rows")) * cells_dev
    band = band_blocks(neighbours, hblocks, first_cell)
    shaped = solutions.reshape((-1,) + solutions.shape[2:])
    applied, ritz = fused(shaped, mixing, band, quads, rows, 1.0 / (rows_dev * quads * rows))
    return (
        applied.reshape(2 * half_cols, rows_dev),
        ritz,
    )


def solution(mesh):
    in_specs = (
        P("quad", None, None, None, "rows"),
        P(),
        P(),
        P(BOTH, None),
        P(BOTH, None, None),
    )
    out_specs = (P(None, BOTH), P("quad", None, None, None))
    return jax.shard_map(
        per_device, mesh=mesh, in_specs=in_specs, out_specs=out_specs, check_vma=False
    )
```

```python
import functools

import jax
import jax.numpy as jnp
from jax import lax
from jax.experimental import pallas as pl
from jax.experimental.pallas import tpu as pltpu
from jax.sharding import PartitionSpec as P

LCOL = 64
QPTS = 32
KMOM = 8
NB = 8
HALO = 2
LC = 16
LINE = 4
BOTH = ("quad", "rows")
NT = (((1,), (1,)), ((), ()))
MESH = pl.DeviceIdType.MESH


def moment_coefficients(angles, qweights):
    order = jnp.arange(KMOM, dtype=jnp.float32)[:, None]
    phase = order * angles[None, :]
    cosine = jnp.cos(phase)
    sine = jnp.sin(phase)
    real_coef = qweights[0][None, :] * cosine - qweights[1][None, :] * sine
    imag_coef = qweights[0][None, :] * sine + qweights[1][None, :] * cosine
    real_rows = jnp.stack([real_coef, -imag_coef], -1)
    imag_rows = jnp.stack([imag_coef, real_coef], -1)
    mixing = jnp.stack([real_rows, imag_rows], 0)
    return mixing.reshape(2 * KMOM, 2 * QPTS).astype(jnp.bfloat16)


def step_plan(quads):
    bits = quads.bit_length() - 1
    rising = [(1 << i, True) for i in range(bits)]
    falling = [(1, True)] + [(1 << i, False) for i in range(bits - 1, 0, -1)]
    return rising, falling


def fused_kernel(
    quads, groups_r, scale, solutions, mixing, neighbours, hblocks, applied, ritz,
    band, outgoing, incoming, passed, landed, moments, low, high, wide, gram, sent, got, last, last_got,
    own_sem, a2a_send, a2a_recv, line_send, line_recv, halo_send, halo_recv, step_send, step_recv, row_send, row_recv,
):
    points, columns, owners, rows = solutions.shape
    chunks = columns // LC
    parts = 2 * KMOM
    half = KMOM * columns
    share = half // quads
    cells, orbitals, reach = band.shape
    pairs, width = cells // 2, 2 * orbitals
    side = low.shape[-1]
    me = lax.axis_index("quad")
    row = lax.axis_index("rows")
    flat = me * groups_r + row
    total = quads * groups_r
    after, before = lax.rem(flat + 1, total), lax.rem(flat + total - 1, total)
    after = {"quad": after // groups_r, "rows": lax.rem(after, groups_r)}
    before = {"quad": before // groups_r, "rows": lax.rem(before, groups_r)}
    row_steps = [1 << i for i in range(groups_r.bit_length() - 1)]

    def partner(index, step):
        return index + step - 2 * step * lax.rem(index // step, 2)

    group = quads // LINE
    spot = lax.rem(me, group)
    line = me // group

    def copy_out(c, o):
        target = lax.rem(spot + o, group)
        return pltpu.make_async_remote_copy(
            src_ref=outgoing.at[c, target],
            dst_ref=incoming.at[c, spot],
            send_sem=a2a_send.at[c, o],
            recv_sem=a2a_recv.at[c, o],
            device_id={"quad": line * group + target},
            device_id_type=MESH,
        )

    def own_copy(c):
        return pltpu.make_async_copy(outgoing.at[c, spot], incoming.at[c, spot], own_sem.at[c])

    def line_copy(c, slot, landing, shift):
        return pltpu.make_async_remote_copy(
            src_ref=passed.at[c, slot],
            dst_ref=landed.at[c, landing],
            send_sem=line_send.at[c, slot],
            recv_sem=line_recv.at[c, landing],
            device_id={"quad": lax.rem(me + shift + quads, quads)},
            device_id_type=MESH,
        )

    size = owners * LC
    r_index = lax.broadcasted_iota(jnp.int32, (size, size), 0)
    c_index = lax.broadcasted_iota(jnp.int32, (size, size), 1)
    swap = jnp.where(
        (lax.rem(r_index // LC, LINE) * group + r_index // (LC * LINE) == lax.rem(c_index, owners)) & (lax.rem(r_index, LC) == c_index // owners), 1.0, 0.0
    ).astype(jnp.bfloat16)

    def rearrange(c):
        def one(q, carry):
            block = solutions[q, c * LC : (c + 1) * LC].reshape(size, rows)
            moved = jnp.dot(swap, block, preferred_element_type=jnp.float32).astype(jnp.bfloat16)
            outgoing[c, :, :, q] = moved.reshape(group, LINE, LC, rows)
            return carry

        lax.fori_loop(0, points, one, 0)

    barrier = pltpu.get_barrier_semaphore()

    near_by = [line * group + lax.rem(spot + o, group) for o in range(1, group)]
    near_by += [lax.rem(me + group, quads), lax.rem(me + quads - group, quads)]
    near_by += [partner(me, 1 << b) for b in range(quads.bit_length() - 1)]
    for other in near_by:
        pl.semaphore_signal(barrier, inc=1, device_id={"quad": other}, device_id_type=MESH)
    pl.semaphore_signal(barrier, inc=1, device_id=after, device_id_type=MESH)
    pl.semaphore_signal(barrier, inc=1, device_id=before, device_id_type=MESH)
    for step in row_steps:
        pl.semaphore_signal(
            barrier, inc=1, device_id={"rows": partner(row, step)}, device_id_type=MESH
        )
    rearrange(0)
    pl.semaphore_wait(barrier, len(near_by) + 2 + len(row_steps))

    for c in range(chunks):
        if c:
            rearrange(c)

        def send(o, carry):
            copy_out(c, o).start()
            return carry

        lax.fori_loop(1, group, send, 0)
        own_copy(c).start()

    high_rows, deep = wide.shape
    spread_p = jnp.where(
        lax.broadcasted_iota(jnp.int32, (high_rows, parts), 0) // LC
        == lax.broadcasted_iota(jnp.int32, (high_rows, parts), 1), 1.0, 0.0,
    ).astype(jnp.bfloat16)
    all_points = mixing.shape[1]
    spread_q = jnp.where(
        lax.broadcasted_iota(jnp.int32, (all_points, deep), 1) // LC + line * (deep // LC)
        == lax.broadcasted_iota(jnp.int32, (all_points, deep), 0), 1.0, 0.0,
    ).astype(jnp.bfloat16)
    tall = jnp.dot(spread_p, mixing[...], preferred_element_type=jnp.float32).astype(jnp.bfloat16)
    full = jnp.dot(tall, spread_q, preferred_element_type=jnp.float32)
    same = lax.rem(lax.broadcasted_iota(jnp.int32, (high_rows, deep), 0), LC) == lax.rem(
        lax.broadcasted_iota(jnp.int32, (high_rows, deep), 1), LC
    )
    wide[...] = jnp.where(same, full, 0.0).astype(jnp.bfloat16)

    first_cell = flat * cells

    def pack_cell(cell, carry):
        base = first_cell - HALO + cell // 2 * 2
        blocks = [
            hblocks[cell, :, n * orbitals : (n + 1) * orbitals].astype(jnp.float32) for n in range(NB)
        ]
        places = [neighbours[cell, n] - base for n in range(NB)]
        chosen = []
        for d in range(2 * HALO + 2):
            summed = jnp.zeros((orbitals, orbitals), jnp.float32)
            for n in range(NB):
                summed = summed + jnp.where(places[n] == d, 1.0, 0.0) * blocks[n]
            chosen.append(summed)
        band[cell] = jnp.concatenate(chosen, -1).astype(jnp.bfloat16)
        return carry

    lax.fori_loop(0, cells, pack_cell, 0)

    def halo_copies(c):
        up = pltpu.make_async_remote_copy(
            src_ref=moments.at[:, c, :, rows - side : rows],
            dst_ref=low.at[:, c],
            send_sem=halo_send.at[0, c],
            recv_sem=halo_recv.at[0, c],
            device_id=after,
            device_id_type=MESH,
        )
        down = pltpu.make_async_remote_copy(
            src_ref=moments.at[:, c, :, 0:side],
            dst_ref=high.at[:, c],
            send_sem=halo_send.at[1, c],
            recv_sem=halo_recv.at[1, c],
            device_id=before,
            device_id_type=MESH,
        )
        return up, down

    def apply_band(c):
        for copy in halo_copies(c):
            copy.wait_recv()
        near = jnp.concatenate([low[:, c], moments[:, c], high[:, c]], -1)
        near = near.reshape(parts * LC, rows + 2 * side)
        for i in range(pairs):
            out = lax.dot_general(
                near[:, i * width : i * width + reach], band[2 * i : 2 * i + 2].reshape(width, reach), NT, preferred_element_type=jnp.float32
            )
            applied[:, c, :, i * width : (i + 1) * width] = out.astype(jnp.bfloat16).reshape(
                parts, LC, width
            )

    def partial_sum(c, slot):
        block = incoming[c, :, slot].reshape(deep, rows)
        return jnp.dot(wide[...], block, preferred_element_type=jnp.float32).reshape(parts, LC, rows)

    def forward(c):
        for slot in list(range(LINE - 1, 0, -1)):

            @pl.when((line == 0) & (slot > 0))
            def _():
                passed[c, slot] = partial_sum(c, slot).astype(jnp.bfloat16)
                line_copy(c, slot, slot, group).start()

            @pl.when((line > 0) & (line < slot))
            def _():
                value = partial_sum(c, slot)
                line_copy(c, slot, slot, group).wait_recv()
                passed[c, slot] = (value + landed[c, slot].astype(jnp.float32)).astype(jnp.bfloat16)
                line_copy(c, slot, slot, group).start()

        for slot in range(LINE - 1):

            @pl.when(line > slot)
            def _():
                value = partial_sum(c, slot)

                @pl.when(line == LINE - 1)
                def _():
                    passed[c, slot] = value.astype(jnp.bfloat16)

                @pl.when(line < LINE - 1)
                def _():
                    line_copy(c, slot, slot, -group).wait_recv()
                    passed[c, slot] = (value + landed[c, slot].astype(jnp.float32)).astype(jnp.bfloat16)

                landing = jnp.where(line - 1 == slot, LINE, slot)
                line_copy(c, slot, landing, -group).start()

    def finish(c):
        base = partial_sum(c, line)

        @pl.when(line == 0)
        def _():
            line_copy(c, 0, LINE, -group).wait_recv()
            moments[:, c] = (base + landed[c, LINE].astype(jnp.float32)).astype(jnp.bfloat16)

        @pl.when(line == LINE - 1)
        def _():
            line_copy(c, 0, LINE - 1, group).wait_recv()
            moments[:, c] = (base + landed[c, LINE - 1].astype(jnp.float32)).astype(jnp.bfloat16)

        @pl.when((line > 0) & (line < LINE - 1))
        def _():
            line_copy(c, 0, line, group).wait_recv()
            line_copy(c, 0, LINE, -group).wait_recv()
            both = landed[c, line].astype(jnp.float32) + landed[c, LINE].astype(jnp.float32)
            moments[:, c] = (base + both).astype(jnp.bfloat16)

        for copy in halo_copies(c):
            copy.start()

    for c in range(chunks):
        own_copy(c).wait()

        def arrive(o, carry):
            copy_out(c, o).wait_recv()
            return carry

        lax.fori_loop(1, group, arrive, 0)
        forward(c)
        if c:
            finish(c - 1)
        if c > 1:
            apply_band(c - 2)
    finish(chunks - 1)
    apply_band(chunks - 2)

    def prod(left, right):
        return lax.dot_general(left, right, NT, preferred_element_type=jnp.float32)

    def grams(m, right):
        real = moments[:KMOM].reshape(half, rows)
        imag = moments[KMOM:].reshape(half, rows)
        other_real = right[:KMOM].reshape(half, rows)
        other_imag = right[KMOM:].reshape(half, rows)
        plain = prod(real, other_real) + prod(imag, other_imag)
        gram[m, :, :, :half] = plain.reshape(quads, share, half)
        cross = prod(real, other_imag) - prod(imag, other_real)
        gram[m, :, :, half:] = cross.reshape(quads, share, half)

    plans = step_plan(quads)
    steps = len(plans[0])

    def place(s):
        return quads - (quads >> s)

    def step_copy(m, s):
        bit, _ = plans[m][s]
        count = quads >> (s + 1)
        return pltpu.make_async_remote_copy(
            src_ref=sent.at[m, pl.ds(place(s), count)],
            dst_ref=got.at[m, pl.ds(place(s), count)],
            send_sem=step_send.at[m, s],
            recv_sem=step_recv.at[m, s],
            device_id={"quad": partner(me, bit)},
            device_id_type=MESH,
        )

    def position(m, s, j, side_bit):
        _, rising = plans[m][s]
        count = quads >> (s + 1)
        return 2 * j + side_bit if rising else j + side_bit * count

    def pack(m, s):
        bit, _ = plans[m][s]
        mine = lax.rem(me // bit, 2)

        def one(j, carry):
            sent[m, place(s) + j] = gram[m, position(m, s, j, 1 - mine)].astype(jnp.bfloat16)
            return carry

        lax.fori_loop(0, quads >> (s + 1), one, 0)
        step_copy(m, s).start()

    def gather(m, s):
        bit, _ = plans[m][s]
        mine = lax.rem(me // bit, 2)
        step_copy(m, s).wait_recv()

        def one(j, carry):
            gram[m, j] = gram[m, position(m, s, j, mine)] + got[m, place(s) + j].astype(jnp.float32)
            return carry

        lax.fori_loop(0, quads >> (s + 1), one, 0)

    def row_copy(m, s):
        return pltpu.make_async_remote_copy(
            src_ref=last.at[m, s],
            dst_ref=last_got.at[m, s],
            send_sem=row_send.at[m, s],
            recv_sem=row_recv.at[m, s],
            device_id={"rows": partner(row, row_steps[s])},
            device_id_type=MESH,
        )

    grams(0, moments)
    pack(0, 0)
    apply_band(chunks - 1)
    grams(1, applied)
    pack(1, 0)
    for s in range(steps):
        for m in range(2):
            gather(m, s)
            if s + 1 < steps:
                pack(m, s + 1)
            else:
                last[m, 0] = gram[m, 0]
                row_copy(m, 0).start()
    for s in range(len(row_steps)):
        for m in range(2):
            row_copy(m, s).wait_recv()
            summed = last[m, s] + last_got[m, s]
            if s + 1 < len(row_steps):
                last[m, s + 1] = summed
                row_copy(m, s + 1).start()
            else:
                for p in range(2):
                    ritz[:, m, p, :] = summed[:, p * half : (p + 1) * half] * scale

    for c in range(chunks):

        def leave(o, carry):
            copy_out(c, o).wait_send()
            return carry

        lax.fori_loop(1, group, leave, 0)
        for copy in halo_copies(c):
            copy.wait_send()
        for slot in range(LINE):

            @pl.when(line != slot)
            def _():
                line_copy(c, slot, slot, group).wait_send()

    for m in range(2):
        for s in range(steps):
            step_copy(m, s).wait_send()
        for s in range(len(row_steps)):
            row_copy(m, s).wait_send()


def fused(solutions, mixing, neighbours, hblocks, quads, groups_r, scale):
    points, columns, owners, rows = solutions.shape
    chunks = columns // LC
    parts = 2 * KMOM
    half = KMOM * columns
    share = half // quads
    cells, orbitals, _ = hblocks.shape
    side = HALO * orbitals
    group = quads // LINE
    steps = quads.bit_length() - 1
    row_steps = groups_r.bit_length() - 1
    bf, f4 = jnp.bfloat16, jnp.float32
    dma = pltpu.SemaphoreType.DMA
    return pl.pallas_call(
        functools.partial(fused_kernel, quads, groups_r, scale),
        out_shape=(
            jax.ShapeDtypeStruct((parts, chunks, LC, rows), bf),
            jax.ShapeDtypeStruct((share, 2, 2, half), f4),
        ),
        in_specs=[
            pl.BlockSpec(memory_space=pltpu.VMEM),
            pl.BlockSpec(memory_space=pltpu.VMEM),
            pl.BlockSpec(memory_space=pltpu.SMEM),
            pl.BlockSpec(memory_space=pltpu.VMEM),
        ],
        out_specs=(pl.BlockSpec(memory_space=pltpu.VMEM),) * 2,
        scratch_shapes=[
            pltpu.VMEM((cells, orbitals, (2 * HALO + 2) * orbitals), bf),
            pltpu.VMEM((chunks, group, LINE, points, LC, rows), bf),
            pltpu.VMEM((chunks, group, LINE, points, LC, rows), bf),
            pltpu.VMEM((chunks, LINE, parts, LC, rows), bf),
            pltpu.VMEM((chunks, LINE + 1, parts, LC, rows), bf),
            pltpu.VMEM((parts, chunks, LC, rows), bf),
            pltpu.VMEM((parts, chunks, LC, side), bf),
            pltpu.VMEM((parts, chunks, LC, side), bf),
            pltpu.VMEM((parts * LC, group * points * LC), bf),
            pltpu.VMEM((2, quads, share, 2 * half), f4),
            pltpu.VMEM((2, quads, share, 2 * half), bf),
            pltpu.VMEM((2, quads, share, 2 * half), bf),
            pltpu.VMEM((2, row_steps, share, 2 * half), f4),
            pltpu.VMEM((2, row_steps, share, 2 * half), f4),
            dma((chunks,)),
            dma((chunks, group)),
            dma((chunks, group)),
            dma((chunks, LINE)),
            dma((chunks, LINE + 1)),
            dma((2, chunks)),
            dma((2, chunks)),
            dma((2, steps)),
            dma((2, steps)),
            dma((2, row_steps)),
            dma((2, row_steps)),
        ],
        compiler_params=pltpu.CompilerParams(
            collective_id=0, has_side_effects=True, vmem_limit_bytes=56 * 2**20
        ),
    )(solutions, mixing, neighbours, hblocks)


def per_device(solutions, angles, qweights, neighbours, hblocks):
    quads, rows = lax.axis_size("quad"), lax.axis_size("rows")
    rows_dev = solutions.shape[4]
    half_cols = KMOM * LCOL
    mixing = moment_coefficients(angles, qweights)
    shaped = solutions.reshape((-1,) + solutions.shape[2:])
    applied, ritz = fused(shaped, mixing, neighbours, hblocks, quads, rows, 1.0 / (rows_dev * quads * rows))
    return (
        applied.reshape(2 * half_cols, rows_dev),
        ritz,
    )


def solution(mesh):
    in_specs = (
        P("quad", None, None, None, "rows"),
        P(),
        P(),
        P(BOTH, None),
        P(BOTH, None, None),
    )
    out_specs = (P(None, BOTH), P("quad", None, None, None))
    return jax.shard_map(
        per_device, mesh=mesh, in_specs=in_specs, out_specs=out_specs, check_vma=False
    )
```
